32 devices in a mesh: clips: 2 (over x), rows: 16 (over z, y, core).
Axes of the slice: x: 2, y: 2, z: 4, core: 2. Of those that a mesh axis runs over, the one named last changes fastest.
Arguments:
- latents: bfloat16 [8, 64, 160, 384], P('clips', 'rows'), parts along dimension 0, may hold values from -6 to 6
- gamma: float32 [384], replicated, may hold values from 0.5 to 1.5
- weight: bfloat16 [3, 3, 3, 384, 384], replicated, may hold values from -0.0625 to 0.0625
- bias: float32 [384], replicated, may hold values from -3 to 3
- intersection: int32 [32], P('clips'), parts along dimension 0, may hold values from 0 to 2
- ramp: int32 [32], P('clips'), parts along dimension 0, may hold values from 1 to 3
Outputs:
- decoded: bfloat16 [8, 64, 160, 384], P('clips', 'rows'), parts along dimension 0
The draws below stay inside these ranges and needn't reach their ends.
There are 2 independent parts, one for each index of `clips`. The reference program is written for one: setup_inputs(seed, part) draws one part's arguments, and reference() takes and returns one part's arrays. A program takes and returns all parts, laid end to end along the dimension named above; an argument that names none is the same for every part. Nothing has to cross between parts.
All inputs are finite; a program needn't handle non-finite values.
Results may differ from the reference program's by a relative error of at most 0.0034.
Values may be sent and summed in bfloat16 or wider, within the bound.
A program may use at most 448 MiB of HBM per device.

```python
import jax
import jax.numpy as jnp
from jax import lax

C = 384
W = 160
FRAMES = 4
ROWS_DEV = 4
OV_MAX = 2
TILES = 16
H = 64


def with_ends(values, stream_key, smallest, largest):
    shape = values.shape
    index_at = [jax.random.randint(jax.random.fold_in(stream_key, axis), (), 0, shape[axis]) for axis in range(len(shape))]
    values = values.at[tuple(index_at)].set(smallest)
    longest = shape.index(max(shape))
    index_at[longest] = (index_at[longest] + 1) % shape[longest]
    return values.at[tuple(index_at)].set(largest)


def block_scale(stream_key, shape, shards, low, largest):
    factor_of, own = 1.0, jax.random.fold_in(stream_key, 6)
    for position, parts in shards:
        heights = jnp.exp(jax.random.uniform(jax.random.fold_in(own, position), (parts,), jnp.float32, low / len(shards), largest / len(shards)))
        factor_of = factor_of * jnp.repeat(heights, shape[position] // parts).reshape([-1 if axis == position else 1 for axis in range(len(shape))])
    return factor_of


def scatter_about(rng, extent, scale, most, cuts=(), held_as=jnp.bfloat16):
    drawn = jax.random.normal(rng, extent, jnp.float32) * scale
    if len(cuts) > 0:
        drawn = block_scale(rng, extent, cuts, -0.22, 0.18) * drawn
    return jnp.clip(drawn, min=-most, max=most).astype(held_as)


def setup_inputs(seed: int = 0, part: int = 0) -> dict:
    splits = jax.random.split(jax.random.key(seed), 7)
    own_keys = jax.random.split(jax.random.fold_in(splits[6], part), 7)
    return {
        "latents": scatter_about(own_keys[0], (FRAMES, H, W, C), 1.0, 6.0, ((1, 16),)),
        "gamma": jnp.clip(jax.random.uniform(splits[1], (C,), jnp.float32, 0.5, 1.5), 0.5, 1.5),
        "weight": scatter_about(splits[2], (3, 3, 3, C, C), (27 * C) ** -0.5, 0.0625),
        "bias": scatter_about(splits[3], (C,), 0.5, 3.0, (), jnp.float32),
        "intersection": with_ends(jax.random.randint(own_keys[4], (TILES,), 0, OV_MAX + 1), jax.random.fold_in(own_keys[4], 1), 0, OV_MAX).astype(jnp.int32),
        "ramp": with_ends(jax.random.randint(own_keys[5], (TILES,), 1, 4), jax.random.fold_in(own_keys[5], 1), 1, 3).astype(jnp.int32),
    }


def activate(tile, gamma, keep):
    values = tile.astype(jnp.float32)
    square = lax.optimization_barrier(jnp.mean(values * values, axis=-1, keepdims=True))
    normed = values * lax.rsqrt(square + 1e-06) * gamma
    return (jax.nn.silu(normed) * keep).astype(jnp.bfloat16)

def convolve(stacked, weight, bias, count):
    padded = jnp.pad(stacked, ((0, 0), (1, 1), (1, 1), (0, 0)))
    height = stacked.shape[1]
    width = stacked.shape[2]
    total = jnp.zeros((count, height, width, weight.shape[4]), jnp.float32)
    for step_t in range(3):
        for step_h in range(3):
            for step_w in range(3):
                slab = padded[step_t:step_t + count, step_h:step_h + height, step_w:step_w + width]
                total = total + jnp.einsum('fhwc,cd->fhwd', slab, weight[step_t, step_h, step_w], preferred_element_type=jnp.float32)
    return total + bias

def decode_tile(tile, keep, gamma, weight, bias):
    act = activate(tile, gamma, keep)
    stacked = jnp.pad(act, ((2, 0), (0, 0), (0, 0), (0, 0)))
    return (tile.astype(jnp.float32) + convolve(stacked, weight, bias, tile.shape[0])).astype(jnp.bfloat16)

def reference(latents, gamma, weight, bias, intersection, ramp):
    rows = ROWS_DEV
    extra = OV_MAX
    tiles = TILES
    padded = jnp.pad(latents, ((0, 0), (0, extra), (0, 0), (0, 0)))
    numbers = jnp.arange(tiles, dtype=jnp.int32)
    eff = jnp.where(numbers == tiles - 1, 0, intersection).astype(jnp.int32)
    places = jnp.arange(rows + extra, dtype=jnp.int32)

    def one_tile(number):
        tile = lax.dynamic_slice_in_dim(padded, (number * rows).astype(jnp.int32), rows + extra, 1)
        keep = (places < rows + eff[number]).astype(jnp.float32).reshape(1, -1, 1, 1)
        return decode_tile(tile, keep, gamma, weight, bias)
    outs = lax.map(one_tile, numbers)
    own = outs[:, :, :rows]
    ext = outs[:, :, rows:]
    prev_ext = jnp.concatenate([jnp.zeros_like(ext[:1]), ext[:-1]], axis=0)
    prev_ov = jnp.concatenate([jnp.zeros((1,), jnp.int32), eff[:-1]], axis=0)
    prev_ramp = jnp.concatenate([jnp.zeros((1,), jnp.int32), ramp[:-1]], axis=0)
    offsets = jnp.arange(extra, dtype=jnp.int32)
    blend_w = jnp.where(offsets[None, :] < prev_ov[:, None], jnp.maximum(prev_ramp[:, None] - offsets[None, :], 0).astype(jnp.float32) / (prev_ramp[:, None] + 1).astype(jnp.float32), jnp.float32(0.0)).astype(jnp.float32)
    blend_w = blend_w.reshape(tiles, 1, extra, 1, 1)
    head = own[:, :, :extra].astype(jnp.float32)
    mixed = (blend_w * prev_ext.astype(jnp.float32) + (1.0 - blend_w) * head).astype(jnp.bfloat16)
    result = jnp.concatenate([mixed, own[:, :, extra:]], axis=2)
    result = jnp.transpose(result, (1, 0, 2, 3, 4))
    return result.reshape(result.shape[0], tiles * rows, result.shape[3], result.shape[4])
```

```python
import functools

import jax
import jax.numpy as jnp
from jax import lax
from jax.experimental import pallas as pl
from jax.experimental.pallas import tpu as pltpu
from jax.sharding import PartitionSpec as P

TAPS = 3
POINTS = 4
MESH = pl.DeviceIdType.MESH
PAD = 8
LANES = 128
RING = 8

ABOVE, ROW0, ROW1, ROW1S, ROW2, ROW2S, ROW3, BELOW = range(8)
ROW_OF = ((1, 2), (0, 3))
READS = (
    ((ROW0, ROW1, ROW2S), (ROW1, ROW2, ROW3)),
    ((ABOVE, ROW0, ROW1S), (ROW2, ROW3, BELOW)),
)
UNITS = (
    ((0,), (0, 1), ((0, 1),)),
    ((0,), (2,), ((2,),)),
    ((1,), (1,), ((0,),)),
    ((2, 1), (2, 3), ((0, 1), (1, 2))),
    ((3,), (3,), ((0,),)),
)


def kernel(
    frames, width, chans, count,
    x_ref, w_ref, gamma_ref, bias_ref, inter_hbm, ramp_hbm,
    out_ref,
    xbuf, top, bot, wbuf, gbuf, dbuf, act, ybuf, obuf, inter_ref, ramp_ref,
    xsem, wsem, ssem, send_sem, recv_sem,
):
    me = lax.axis_index("rows")
    last = xbuf.shape[1] - 1
    half_w = width // 2

    def x_copy(f):
        return pltpu.make_async_copy(x_ref.at[f], xbuf.at[f], xsem.at[f])

    def w_copy(t, k):
        return pltpu.make_async_copy(
            w_ref.at[TAPS - 1 - t, :, k], wbuf.at[t, :, k], wsem.at[t, k]
        )

    def down(f):
        return pltpu.make_async_remote_copy(
            src_ref=x_ref.at[f, last], dst_ref=top.at[f], send_sem=send_sem.at[0, f],
            recv_sem=recv_sem.at[0, f], device_id={"rows": me + 1}, device_id_type=MESH,
        )

    def up(f):
        return pltpu.make_async_remote_copy(
            src_ref=x_ref.at[f, 0], dst_ref=bot.at[f], send_sem=send_sem.at[1, f],
            recv_sem=recv_sem.at[1, f], device_id={"rows": me - 1}, device_id_type=MESH,
        )

    small = (
        pltpu.make_async_copy(inter_hbm, inter_ref, ssem.at[0]),
        pltpu.make_async_copy(ramp_hbm, ramp_ref, ssem.at[1]),
    )
    barrier = pltpu.get_barrier_semaphore()

    @pl.when(me > 0)
    def _():
        pl.semaphore_signal(
            barrier, inc=1, device_id={"rows": me - 1}, device_id_type=MESH
        )

    @pl.when(me < count - 1)
    def _():
        pl.semaphore_signal(
            barrier, inc=1, device_id={"rows": me + 1}, device_id_type=MESH
        )

    for copy in small:
        copy.start()
    for f in range(frames):
        x_copy(f).start()
    for t, k in ((0, 0), (1, 0), (0, 2), (1, 2), (2, 0), (2, 2), (0, 1), (1, 1), (2, 1)):
        w_copy(t, k).start()

    @pl.when(me == 0)
    def _():
        top[...] = jnp.zeros(top.shape, top.dtype)

    @pl.when(me == count - 1)
    def _():
        bot[...] = jnp.zeros(bot.shape, bot.dtype)

    for b in range(RING):
        for c in range(chans // LANES):
            act[b, c, 0:PAD] = jnp.zeros((PAD, LANES), jnp.float32)
            act[b, c, PAD + width : PAD + width + PAD] = jnp.zeros(
                (PAD, LANES), jnp.float32
            )

    peers = jnp.where(me > 0, 1, 0) + jnp.where(me < count - 1, 1, 0)
    pl.semaphore_wait(barrier, peers)

    @pl.when(me < count - 1)
    def _():
        for f in range(frames):
            down(f).start()

    @pl.when(me > 0)
    def _():
        for f in range(frames):
            up(f).start()

    for copy in small:
        copy.wait()

    before = jnp.maximum(me - 1, 0)
    prev_ov = jnp.where(me > 0, inter_ref[before], 0)
    own_ov = jnp.where(me == count - 1, 0, inter_ref[me])
    ovv = jnp.full((1, chans), prev_ov, jnp.int32)
    ownv = jnp.full((1, chans), own_ov, jnp.int32)
    rampv = jnp.full((1, chans), ramp_ref[before], jnp.int32).astype(jnp.float32)
    a0 = jnp.where(ovv > 0, jnp.maximum(rampv, 0.0) / (rampv + 1.0), 0.0)
    a1 = jnp.where(ovv > 1, jnp.maximum(rampv - 1.0, 0.0) / (rampv + 1.0), 0.0)
    s1 = jnp.where(ovv > 1, 1.0, 1.0 - a0)
    s2 = 1.0 - a1
    live = jnp.where(ownv > 0, 1.0, 0.0)
    half_gamma = 0.5 * gamma_ref[...].reshape(1, chans)
    bias = bias_ref[...].reshape(1, chans)
    ring = [0]

    def activate(f, source, targets):
        values = source.astype(jnp.float32)
        square = jnp.mean(values * values, axis=-1, keepdims=True)
        half = values * lax.rsqrt(square + 1e-06) * half_gamma
        b = ring[0] % RING
        ring[0] += 1
        value = half + half * jnp.tanh(half)
        for c in range(chans // LANES):
            lanes = slice(c * LANES, (c + 1) * LANES)
            act[b, c, PAD : PAD + width] = value[:, lanes]
            parts = [
                act[b, c, pl.ds(PAD + at, half_w, stride=2)] for at in (-1, 0, 1, 2)
            ]
            for version, scale in targets:
                odd_b, even, odd, even_a = [
                    (part if scale is None else part * scale[:, lanes]).astype(
                        jnp.bfloat16
                    )
                    for part in parts
                ]
                dbuf[0, f, version, :, lanes] = odd_b - odd
                dbuf[1, f, version, :, lanes] = even + odd
                dbuf[2, f, version, :, lanes] = odd - even
                dbuf[3, f, version, :, lanes] = even - even_a

    own_targets = (
        ((ROW0, None),),
        ((ROW1, None), (ROW1S, s1)),
        ((ROW2, None), (ROW2S, s2)),
        ((ROW3, None),),
    )

    def own(f, row):
        activate(f, xbuf[f, row], own_targets[row])

    def edge(f):
        activate(f, top[f], ((ABOVE, a0),))
        activate(f, bot[f], ((BELOW, live),))

    def add_weights(t, h):
        g0, g1, g2 = [wbuf[t, h, k].astype(jnp.float32) for k in range(TAPS)]
        both = g0 + g2
        gbuf[0, t, h] = (both + g1).astype(jnp.bfloat16)
        gbuf[1, t, h] = (both - g1).astype(jnp.bfloat16)

    def filters(p, t):
        if p in (0, 3):
            k = 0 if p == 0 else TAPS - 1
            return jnp.concatenate([wbuf[t, h, k] for h in range(TAPS)], axis=0)
        return jnp.concatenate([gbuf[p - 1, t, h] for h in range(TAPS)], axis=0)

    written = set()

    def multiply(half, unit, p):
        sources, outputs, taps = UNITS[unit]
        left = jnp.concatenate(
            [
                jnp.concatenate(
                    [dbuf[p, f, version] for f in sources for version in reads], axis=1
                )
                for reads in READS[half]
            ],
            axis=0,
        )
        right = jnp.concatenate(
            [
                jnp.concatenate([filters(p, t) for t in across], axis=1)
                if len(across) > 1 else filters(p, across[0])
                for across in taps
            ],
            axis=0,
        )
        product = jnp.dot(left, right, preferred_element_type=jnp.float32)
        for n, o in enumerate(outputs):
            part = product[:, n * chans : (n + 1) * chans]
            if (half, o, p) in written:
                ybuf[half, o, p] += part
            else:
                ybuf[half, o, p] = part
                written.add((half, o, p))

    oring = [0]

    def finish(half, f):
        for slot in range(2):
            row = ROW_OF[half][slot]
            y0, y1, y2, y3 = [
                ybuf[half, f, p, slot * half_w : (slot + 1) * half_w]
                for p in range(POINTS)
            ]
            b = oring[0] % RING
            oring[0] += 1
            even = y0 + 0.5 * (y1 + y2)
            odd = 0.5 * (y1 - y2) - y3
            for c in range(chans // LANES):
                lanes = slice(c * LANES, (c + 1) * LANES)
                obuf[b, c, pl.ds(0, half_w, stride=2)] = even[:, lanes]
                obuf[b, c, pl.ds(1, half_w, stride=2)] = odd[:, lanes]
                total = obuf[b, c] + (
                    xbuf[f, row, :, lanes].astype(jnp.float32) + bias[:, lanes]
                )
                out_ref[f, row, :, lanes] = total.astype(jnp.bfloat16)

    rows = range(last + 1)
    x_copy(0).wait()
    for row in rows:
        own(0, row)
    for f in range(1, frames):
        x_copy(f).wait()
    for t, k in ((0, 0), (1, 0), (0, 2), (1, 2)):
        w_copy(t, k).wait()
    multiply(0, 0, 0)
    for row in rows:
        own(1, row)
    multiply(0, 0, 3)
    for t, k in ((2, 0), (2, 2), (0, 1), (1, 1), (2, 1)):
        w_copy(t, k).wait()
    multiply(0, 1, 0)
    own(2, 0)
    own(2, 1)
    multiply(0, 1, 3)
    own(2, 2)
    own(2, 3)
    multiply(0, 2, 0)
    add_weights(0, 0)
    multiply(0, 2, 3)
    add_weights(0, 1)
    multiply(0, 3, 0)
    for row in rows:
        own(3, row)
    multiply(0, 3, 3)
    add_weights(0, 2)
    multiply(0, 4, 0)
    add_weights(1, 0)
    multiply(0, 4, 3)
    multiply(0, 2, 1)
    add_weights(1, 1)
    multiply(0, 2, 2)
    multiply(0, 4, 1)
    add_weights(1, 2)
    multiply(0, 4, 2)
    multiply(0, 0, 1)
    add_weights(2, 0)
    multiply(0, 0, 2)
    finish(0, 0)
    finish(0, 1)
    add_weights(2, 1)
    add_weights(2, 2)
    multiply(0, 1, 1)
    multiply(0, 1, 2)

    def arrived(f):
        @pl.when(me > 0)
        def _():
            down(f).wait_recv()

        @pl.when(me < count - 1)
        def _():
            up(f).wait_recv()

    arrived(0)
    multiply(0, 3, 1)
    edge(0)
    multiply(0, 3, 2)
    arrived(1)
    for p in range(POINTS):
        multiply(1, 0, p)
        if p == 0:
            edge(1)
    finish(0, 2)
    finish(0, 3)
    for p in range(POINTS):
        multiply(1, 1, p)
    arrived(2)
    for p in range(POINTS):
        multiply(1, 2, p)
        if p == 0:
            edge(2)
    finish(1, 0)
    finish(1, 1)
    for p in range(POINTS):
        multiply(1, 3, p)
    arrived(3)
    edge(3)
    finish(1, 2)
    for p in range(POINTS):
        multiply(1, 4, p)
    finish(1, 3)

    @pl.when(me < count - 1)
    def _():
        for f in range(frames):
            down(f).wait_send()

    @pl.when(me > 0)
    def _():
        for f in range(frames):
            up(f).wait_send()


def hand_on(frames, held, to_ref, sem):
    copies = [
        pltpu.make_async_copy(held.at[f], to_ref.at[f], sem.at[f])
        for f in range(frames)
    ]
    for copy in copies:
        copy.start()
    for copy in copies:
        copy.wait()


def per_device(latents, gamma, weight, bias, intersection, ramp):
    frames, rows, width, chans = latents.shape
    count = lax.axis_size("rows")
    hbm = pl.BlockSpec(memory_space=pltpu.HBM)
    vmem = pl.BlockSpec(memory_space=pltpu.VMEM)
    made = pl.pallas_call(
        functools.partial(kernel, frames, width, chans, count),
        out_shape=pltpu.VMEM(latents.shape, latents.dtype),
        in_specs=[hbm, hbm, vmem, vmem, hbm, hbm],
        out_specs=vmem,
        scratch_shapes=[
            pltpu.VMEM((frames, rows, width, chans), jnp.bfloat16),
            pltpu.VMEM((frames, width, chans), jnp.bfloat16),
            pltpu.VMEM((frames, width, chans), jnp.bfloat16),
            pltpu.VMEM((TAPS, TAPS, TAPS, chans, chans), jnp.bfloat16),
            pltpu.VMEM((2, TAPS, TAPS, chans, chans), jnp.bfloat16),
            pltpu.VMEM((POINTS, frames, 8, width // 2, chans), jnp.bfloat16),
            pltpu.VMEM((RING, chans // LANES, width + 2 * PAD, LANES), jnp.float32),
            pltpu.VMEM((2, frames, POINTS, width, chans), jnp.float32),
            pltpu.VMEM((RING, chans // LANES, width, LANES), jnp.float32),
            pltpu.SMEM(intersection.shape, jnp.int32),
            pltpu.SMEM(ramp.shape, jnp.int32),
            pltpu.SemaphoreType.DMA((frames,)),
            pltpu.SemaphoreType.DMA((TAPS, TAPS)),
            pltpu.SemaphoreType.DMA((2,)),
            pltpu.SemaphoreType.DMA((2, frames)),
            pltpu.SemaphoreType.DMA((2, frames)),
        ],
        compiler_params=pltpu.CompilerParams(
            collective_id=0, has_side_effects=True, vmem_limit_bytes=56 * 1024 * 1024
        ),
    )(latents, weight, gamma, bias, intersection, ramp)
    return pl.pallas_call(
        functools.partial(hand_on, frames),
        out_shape=jax.ShapeDtypeStruct(latents.shape, latents.dtype),
        in_specs=[vmem],
        out_specs=hbm,
        scratch_shapes=[pltpu.SemaphoreType.DMA((frames,))],
        compiler_params=pltpu.CompilerParams(vmem_limit_bytes=16 * 1024 * 1024),
    )(made)


def solution(mesh):
    in_specs = (P("clips", "rows", None, None), P(), P(), P(), P("clips"), P("clips"))
    out_specs = P("clips", "rows", None, None)
    return jax.shard_map(
        per_device, mesh=mesh, in_specs=in_specs, out_specs=out_specs, check_vma=False
    )
```

```python
import functools

import jax
import jax.numpy as jnp
from jax import lax
from jax.experimental import pallas as pl
from jax.experimental.pallas import tpu as pltpu
from jax.sharding import PartitionSpec as P

TAPS = 3
POINTS = 4
MESH = pl.DeviceIdType.MESH
PAD = 8
LANES = 128
RING = 8

ABOVE, ROW0, ROW1, ROW1S, ROW2, ROW2S, ROW3, BELOW = range(8)
ROW_OF = ((1, 2), (0, 3))
READS = (
    ((ROW0, ROW1, ROW2S), (ROW1, ROW2, ROW3)),
    ((ABOVE, ROW0, ROW1S), (ROW2, ROW3, BELOW)),
)
UNITS = (
    ((1, 0), (1, 2), ((0, 1), (1, 2))),
    ((2,), (2, 3), ((0, 1),)),
    ((0,), (0,), ((0,),)),
    ((1, 3), (3,), ((2,), (0,))),
)
A, B, C, D = range(4)
STEP = 32
DEEP = 64
EARLY = ((0, 0), (0, 2), (1, 0), (1, 2))
LATE = ((2, 0), (2, 2), (0, 1), (1, 1), (2, 1))


def kernel(
    frames, width, chans, count,
    x_ref, w_ref, gamma_hbm, bias_hbm, inter_hbm, ramp_hbm,
    out_ref,
    xbuf, top, bot, wbuf, gbuf, dbuf, act, ybuf, obuf, gamma_ref, bias_ref, inter_ref, ramp_ref,
    xsem, wsem, ssem, send_sem, recv_sem,
):
    me = lax.axis_index("rows")
    last = xbuf.shape[1] - 1
    half_w = width // 2

    def x_copy(f):
        return pltpu.make_async_copy(x_ref.at[f], xbuf.at[f], xsem.at[f])

    def w_copy(t, k):
        return pltpu.make_async_copy(
            w_ref.at[TAPS - 1 - t, :, k], wbuf.at[t, :, k], wsem.at[t, k]
        )

    def down(f):
        return pltpu.make_async_remote_copy(
            src_ref=x_ref.at[f, last], dst_ref=top.at[f], send_sem=send_sem.at[0, f],
            recv_sem=recv_sem.at[0, f], device_id={"rows": me + 1}, device_id_type=MESH,
        )

    def up(f):
        return pltpu.make_async_remote_copy(
            src_ref=x_ref.at[f, 0], dst_ref=bot.at[f], send_sem=send_sem.at[1, f],
            recv_sem=recv_sem.at[1, f], device_id={"rows": me - 1}, device_id_type=MESH,
        )

    small = (
        pltpu.make_async_copy(inter_hbm, inter_ref, ssem.at[0]),
        pltpu.make_async_copy(ramp_hbm, ramp_ref, ssem.at[1]),
        pltpu.make_async_copy(gamma_hbm, gamma_ref, ssem.at[2]),
        pltpu.make_async_copy(bias_hbm, bias_ref, ssem.at[3]),
    )
    barrier = pltpu.get_barrier_semaphore()

    @pl.when(me > 0)
    def _():
        pl.semaphore_signal(
            barrier, inc=1, device_id={"rows": me - 1}, device_id_type=MESH
        )

    @pl.when(me < count - 1)
    def _():
        pl.semaphore_signal(
            barrier, inc=1, device_id={"rows": me + 1}, device_id_type=MESH
        )

    for copy in small:
        copy.start()
    for f in range(frames):
        x_copy(f).start()
    for t, k in EARLY + LATE:
        w_copy(t, k).start()

    @pl.when(me == 0)
    def _():
        top[...] = jnp.zeros(top.shape, top.dtype)

    @pl.when(me == count - 1)
    def _():
        bot[...] = jnp.zeros(bot.shape, bot.dtype)

    for b in range(RING):
        for c in range(chans // LANES):
            act[b, c, 0:PAD] = jnp.zeros((PAD, LANES), jnp.float32)
            act[b, c, PAD + width : PAD + width + PAD] = jnp.zeros(
                (PAD, LANES), jnp.float32
            )

    peers = jnp.where(me > 0, 1, 0) + jnp.where(me < count - 1, 1, 0)
    pl.semaphore_wait(barrier, peers)

    for f in range(frames):

        @pl.when(me < count - 1)
        def _():
            down(f).start()

        @pl.when(me > 0)
        def _():
            up(f).start()

    for copy in small:
        copy.wait()

    before = jnp.maximum(me - 1, 0)
    prev_ov = jnp.where(me > 0, inter_ref[before], 0)
    own_ov = jnp.where(me == count - 1, 0, inter_ref[me])
    ovv = jnp.full((1, chans), prev_ov, jnp.int32)
    ownv = jnp.full((1, chans), own_ov, jnp.int32)
    rampv = jnp.full((1, chans), ramp_ref[before], jnp.int32).astype(jnp.float32)
    a0 = jnp.where(ovv > 0, jnp.maximum(rampv, 0.0) / (rampv + 1.0), 0.0)
    a1 = jnp.where(ovv > 1, jnp.maximum(rampv - 1.0, 0.0) / (rampv + 1.0), 0.0)
    s1 = jnp.where(ovv > 1, 1.0, 1.0 - a0)
    s2 = 1.0 - a1
    live = jnp.where(ownv > 0, 1.0, 0.0)
    half_gamma = 0.5 * gamma_ref[...].reshape(1, chans)
    bias = bias_ref[...].reshape(1, chans)
    ring = [0]

    def activate(f, source, targets):
        b = ring[0] % RING
        ring[0] += 1
        for w0 in range(0, width, STEP):
            values = source[w0 : w0 + STEP].astype(jnp.float32)
            square = jnp.mean(values * values, axis=-1, keepdims=True)
            half = values * lax.rsqrt(square + 1e-06) * half_gamma
            value = half + half * jnp.tanh(half)
            for c in range(chans // LANES):
                lanes = slice(c * LANES, (c + 1) * LANES)
                act[b, c, PAD + w0 : PAD + w0 + STEP] = value[:, lanes]
        for c in range(chans // LANES):
            lanes = slice(c * LANES, (c + 1) * LANES)
            for version, scale in targets:

                def part(at):
                    one = act[b, c, pl.ds(PAD + at, half_w, stride=2)]
                    if scale is not None:
                        one = one * scale[:, lanes]
                    return one.astype(jnp.bfloat16)

                odd = part(1)
                dbuf[0, f, version, c] = part(-1) - odd
                even = part(0)
                dbuf[1, f, version, c] = even + odd
                dbuf[2, f, version, c] = odd - even
                dbuf[3, f, version, c] = even - part(2)

    own_targets = (
        ((ROW0, None),),
        ((ROW1, None), (ROW1S, s1)),
        ((ROW2, None), (ROW2S, s2)),
        ((ROW3, None),),
    )

    def own(f, row):
        activate(f, xbuf.at[f, row], own_targets[row])

    def edge(f):
        activate(f, top.at[f], ((ABOVE, a0),))
        activate(f, bot.at[f], ((BELOW, live),))

    def add_weights(t, h):
        for c in range(chans // LANES):
            lanes = slice(c * LANES, (c + 1) * LANES)
            for r0 in range(0, chans, DEEP):
                at = slice(r0, r0 + DEEP)
                first, middle, final = [
                    wbuf[t, h, k, at, lanes].astype(jnp.float32) for k in range(TAPS)
                ]
                both = first + final
                gbuf[0, t, h, c, at] = (both + middle).astype(jnp.bfloat16)
                gbuf[1, t, h, c, at] = (both - middle).astype(jnp.bfloat16)

    def across_lanes(ref):
        return jnp.concatenate([ref[c] for c in range(chans // LANES)], axis=1)

    def filters(p, t):
        if p in (0, 3):
            k = 0 if p == 0 else TAPS - 1
            return jnp.concatenate([wbuf[t, h, k] for h in range(TAPS)], axis=0)
        return jnp.concatenate(
            [across_lanes(gbuf.at[p - 1, t, h]) for h in range(TAPS)], axis=0
        )

    written = set()

    def multiply(half, unit, p):
        sources, outputs, taps = UNITS[unit]
        left = jnp.concatenate(
            [
                jnp.concatenate(
                    [
                        across_lanes(dbuf.at[p, f, version])
                        for f in sources
                        for version in reads
                    ],
                    axis=1,
                )
                for reads in READS[half]
            ],
            axis=0,
        )
        right = jnp.concatenate(
            [
                jnp.concatenate([filters(p, t) for t in across], axis=1)
                if len(across) > 1 else filters(p, across[0])
                for across in taps
            ],
            axis=0,
        )
        product = jnp.dot(left, right, preferred_element_type=jnp.float32)
        for n, o in enumerate(outputs):
            part = product[:, n * chans : (n + 1) * chans]
            if (half, o, p) in written:
                ybuf[half, o, p] += part
            else:
                ybuf[half, o, p] = part
                written.add((half, o, p))

    oring = [0]

    def finish(half, f):
        for slot in range(2):
            row = ROW_OF[half][slot]
            b = oring[0] % RING
            oring[0] += 1
            at = slice(slot * half_w, (slot + 1) * half_w)
            for c in range(chans // LANES):
                lanes = slice(c * LANES, (c + 1) * LANES)
                y1, y2 = ybuf[half, f, 1, at, lanes], ybuf[half, f, 2, at, lanes]
                obuf[b, c, pl.ds(0, half_w, stride=2)] = (
                    ybuf[half, f, 0, at, lanes] + 0.5 * (y1 + y2)
                )
                obuf[b, c, pl.ds(1, half_w, stride=2)] = (
                    0.5 * (y1 - y2) - ybuf[half, f, 3, at, lanes]
                )
                total = obuf[b, c] + (
                    xbuf[f, row, :, lanes].astype(jnp.float32) + bias[:, lanes]
                )
                out_ref[f, row, :, lanes] = total.astype(jnp.bfloat16)

    rows = range(last + 1)

    def arrived(f):
        @pl.when(me > 0)
        def _():
            down(f).wait_recv()

        @pl.when(me < count - 1)
        def _():
            up(f).wait_recv()

    for f in range(2):
        x_copy(f).wait()
        for row in rows:
            own(f, row)
    for f in range(2, frames):
        x_copy(f).wait()
    for t, k in EARLY:
        w_copy(t, k).wait()
    multiply(0, C, 0)
    own(2, 0)
    own(2, 1)
    multiply(0, C, 3)
    own(2, 2)
    own(2, 3)
    multiply(0, B, 0)
    multiply(0, B, 3)
    for t, k in LATE:
        w_copy(t, k).wait()
    multiply(0, A, 0)
    own(3, 0)
    own(3, 1)
    own(3, 2)
    own(3, 3)
    multiply(0, A, 3)
    for h in range(TAPS):
        add_weights(0, h)
    multiply(0, D, 0)
    add_weights(1, 0)
    multiply(0, D, 3)
    add_weights(1, 1)
    multiply(0, C, 1)
    add_weights(1, 2)
    multiply(0, C, 2)
    add_weights(2, 0)
    multiply(0, B, 1)
    add_weights(2, 1)
    multiply(0, B, 2)
    add_weights(2, 2)
    finish(0, 0)
    multiply(0, A, 1)
    multiply(0, A, 2)
    finish(0, 1)
    arrived(0)
    arrived(1)
    multiply(0, D, 1)
    edge(0)
    multiply(0, D, 2)
    for p in range(POINTS):
        multiply(1, C, p)
    edge(1)
    finish(0, 2)
    multiply(1, A, 0)
    finish(0, 3)
    multiply(1, A, 1)
    finish(1, 0)
    multiply(1, A, 2)
    arrived(2)
    arrived(3)
    multiply(1, A, 3)
    edge(2)
    edge(3)
    multiply(1, B, 0)
    multiply(1, B, 1)
    finish(1, 1)
    multiply(1, B, 2)
    multiply(1, B, 3)
    multiply(1, D, 0)
    finish(1, 2)
    multiply(1, D, 1)
    multiply(1, D, 2)
    multiply(1, D, 3)
    finish(1, 3)

    @pl.when(me < count - 1)
    def _():
        for f in range(frames):
            down(f).wait_send()

    @pl.when(me > 0)
    def _():
        for f in range(frames):
            up(f).wait_send()


def hand_on(frames, held, to_ref, sem):
    copies = [
        pltpu.make_async_copy(held.at[f], to_ref.at[f], sem.at[f])
        for f in range(frames)
    ]
    for copy in copies:
        copy.start()
    for copy in copies:
        copy.wait()


def per_device(latents, gamma, weight, bias, intersection, ramp):
    frames, rows, width, chans = latents.shape
    count = lax.axis_size("rows")
    hbm = pl.BlockSpec(memory_space=pltpu.HBM)
    vmem = pl.BlockSpec(memory_space=pltpu.VMEM)
    made = pl.pallas_call(
        functools.partial(kernel, frames, width, chans, count),
        out_shape=pltpu.VMEM(latents.shape, latents.dtype),
        in_specs=[hbm] * 6,
        out_specs=vmem,
        scratch_shapes=[
            pltpu.VMEM((frames, rows, width, chans), jnp.bfloat16),
            pltpu.VMEM((frames, width, chans), jnp.bfloat16),
            pltpu.VMEM((frames, width, chans), jnp.bfloat16),
            pltpu.VMEM((TAPS, TAPS, TAPS, chans, chans), jnp.bfloat16),
            pltpu.VMEM((2, TAPS, TAPS, chans // LANES, chans, LANES), jnp.bfloat16),
            pltpu.VMEM(
                (POINTS, frames, 8, chans // LANES, width // 2, LANES), jnp.bfloat16
            ),
            pltpu.VMEM((RING, chans // LANES, width + 2 * PAD, LANES), jnp.float32),
            pltpu.VMEM((2, frames, POINTS, width, chans), jnp.float32),
            pltpu.VMEM((RING, chans // LANES, width, LANES), jnp.float32),
            pltpu.VMEM(gamma.shape, jnp.float32),
            pltpu.VMEM(bias.shape, jnp.float32),
            pltpu.SMEM(intersection.shape, jnp.int32),
            pltpu.SMEM(ramp.shape, jnp.int32),
            pltpu.SemaphoreType.DMA((frames,)),
            pltpu.SemaphoreType.DMA((TAPS, TAPS)),
            pltpu.SemaphoreType.DMA((4,)),
            pltpu.SemaphoreType.DMA((2, frames)),
            pltpu.SemaphoreType.DMA((2, frames)),
        ],
        compiler_params=pltpu.CompilerParams(
            collective_id=0, has_side_effects=True, vmem_limit_bytes=56 * 1024 * 1024
        ),
    )(latents, weight, gamma, bias, intersection, ramp)
    return pl.pallas_call(
        functools.partial(hand_on, frames),
        out_shape=jax.ShapeDtypeStruct(latents.shape, latents.dtype),
        in_specs=[vmem],
        out_specs=hbm,
        scratch_shapes=[pltpu.SemaphoreType.DMA((frames,))],
        compiler_params=pltpu.CompilerParams(vmem_limit_bytes=16 * 1024 * 1024),
    )(made)


def solution(mesh):
    in_specs = (P("clips", "rows", None, None), P(), P(), P(), P("clips"), P("clips"))
    out_specs = P("clips", "rows", None, None)
    return jax.shard_map(
        per_device, mesh=mesh, in_specs=in_specs, out_specs=out_specs, check_vma=False
    )
```

```python
import functools

import jax
import jax.numpy as jnp
from jax import lax
from jax.experimental import pallas as pl
from jax.experimental.pallas import tpu as pltpu
from jax.sharding import PartitionSpec as P

TAPS = 3
POINTS = 4
MESH = pl.DeviceIdType.MESH
PAD = 8
LANES = 128
RING = 8

ABOVE, ROW0, ROW1, ROW1S, ROW2, ROW2S, ROW3, BELOW = range(8)
ROW_OF = ((1, 2), (0, 3))
READS = (
    ((ROW0, ROW1, ROW2S), (ROW1, ROW2, ROW3)),
    ((ABOVE, ROW0, ROW1S), (ROW2, ROW3, BELOW)),
)
UNITS = (
    ((1, 0), (1, 2), ((0, 1), (1, 2))),
    ((2,), (2, 3), ((0, 1),)),
    ((0,), (0,), ((0,),)),
    ((1, 3), (3,), ((2,), (0,))),
)
A, B, C, D = range(4)
STEP = 32
DEEP = 64
XPARTS = (pl.ds(0, 1), pl.ds(1, 1), pl.ds(2, 2))
WPARTS = (
    (pl.ds(1, 2), 0), (pl.ds(1, 2), 2), (pl.ds(0, 1), 0), (pl.ds(0, 1), 2),
    (pl.ds(0, TAPS), 1),
)
PAIR = 2


def kernel(
    frames, width, chans, count,
    x_ref, w_ref, gamma_hbm, bias_hbm, inter_hbm, ramp_hbm,
    out_ref,
    xbuf, top, bot, wbuf, gbuf, dbuf, act, ybuf, obuf, gamma_ref, bias_ref, inter_ref, ramp_ref,
    xsem, wsem, ssem, send_sem, recv_sem,
):
    me = lax.axis_index("rows")
    last = xbuf.shape[1] - 1
    half_w = width // 2

    def x_copy(n):
        at = XPARTS[n]
        return pltpu.make_async_copy(x_ref.at[at], xbuf.at[at], xsem.at[n])

    def w_copy(n):
        t, k = WPARTS[n]
        return pltpu.make_async_copy(w_ref.at[t, :, k], wbuf.at[t, :, k], wsem.at[n])

    def down(n):
        at = pl.ds(n * PAIR, PAIR)
        return pltpu.make_async_remote_copy(
            src_ref=x_ref.at[at, last], dst_ref=top.at[at],
            send_sem=send_sem.at[0, n], recv_sem=recv_sem.at[0, n],
            device_id={"rows": me + 1}, device_id_type=MESH,
        )

    def up(n):
        at = pl.ds(n * PAIR, PAIR)
        return pltpu.make_async_remote_copy(
            src_ref=x_ref.at[at, 0], dst_ref=bot.at[at],
            send_sem=send_sem.at[1, n], recv_sem=recv_sem.at[1, n],
            device_id={"rows": me - 1}, device_id_type=MESH,
        )

    small = (
        pltpu.make_async_copy(inter_hbm, inter_ref, ssem.at[0]),
        pltpu.make_async_copy(ramp_hbm, ramp_ref, ssem.at[1]),
        pltpu.make_async_copy(gamma_hbm, gamma_ref, ssem.at[2]),
        pltpu.make_async_copy(bias_hbm, bias_ref, ssem.at[3]),
    )
    barrier = pltpu.get_barrier_semaphore()

    @pl.when(me > 0)
    def _():
        pl.semaphore_signal(
            barrier, inc=1, device_id={"rows": me - 1}, device_id_type=MESH
        )

    @pl.when(me < count - 1)
    def _():
        pl.semaphore_signal(
            barrier, inc=1, device_id={"rows": me + 1}, device_id_type=MESH
        )

    for copy in small:
        copy.start()
    for n in range(len(XPARTS)):
        x_copy(n).start()
    for n in range(len(WPARTS)):
        w_copy(n).start()

    @pl.when(me == 0)
    def _():
        top[...] = jnp.zeros(top.shape, top.dtype)

    @pl.when(me == count - 1)
    def _():
        bot[...] = jnp.zeros(bot.shape, bot.dtype)

    for b in range(RING):
        for c in range(chans // LANES):
            act[b, c, 0:PAD] = jnp.zeros((PAD, LANES), jnp.float32)
            act[b, c, PAD + width : PAD + width + PAD] = jnp.zeros(
                (PAD, LANES), jnp.float32
            )

    peers = jnp.where(me > 0, 1, 0) + jnp.where(me < count - 1, 1, 0)
    pl.semaphore_wait(barrier, peers)

    for n in range(frames // PAIR):

        @pl.when(me < count - 1)
        def _():
            down(n).start()

        @pl.when(me > 0)
        def _():
            up(n).start()

    for copy in small:
        copy.wait()

    before = jnp.maximum(me - 1, 0)
    prev_ov = jnp.where(me > 0, inter_ref[before], 0)
    own_ov = jnp.where(me == count - 1, 0, inter_ref[me])
    ovv = jnp.full((1, chans), prev_ov, jnp.int32)
    ownv = jnp.full((1, chans), own_ov, jnp.int32)
    rampv = jnp.full((1, chans), ramp_ref[before], jnp.int32).astype(jnp.float32)
    a0 = jnp.where(ovv > 0, jnp.maximum(rampv, 0.0) / (rampv + 1.0), 0.0)
    a1 = jnp.where(ovv > 1, jnp.maximum(rampv - 1.0, 0.0) / (rampv + 1.0), 0.0)
    s1 = jnp.where(ovv > 1, 1.0, 1.0 - a0)
    s2 = 1.0 - a1
    live = jnp.where(ownv > 0, 1.0, 0.0)
    half_gamma = 0.5 * gamma_ref[...].reshape(1, chans)
    bias = bias_ref[...].reshape(1, chans)
    ring = [0]

    def activate(f, source, targets):
        b = ring[0] % RING
        ring[0] += 1
        for w0 in range(0, width, STEP):
            values = source[w0 : w0 + STEP].astype(jnp.float32)
            square = jnp.mean(values * values, axis=-1, keepdims=True)
            half = values * lax.rsqrt(square + 1e-06) * half_gamma
            value = half + half * jnp.tanh(half)
            for c in range(chans // LANES):
                lanes = slice(c * LANES, (c + 1) * LANES)
                act[b, c, PAD + w0 : PAD + w0 + STEP] = value[:, lanes]
        for c in range(chans // LANES):
            lanes = slice(c * LANES, (c + 1) * LANES)
            for version, scale in targets:

                def part(at):
                    one = act[b, c, pl.ds(PAD + at, half_w, stride=2)]
                    if scale is not None:
                        one = one * scale[:, lanes]
                    return one.astype(jnp.bfloat16)

                odd = part(1)
                dbuf[0, f, version, c] = part(-1) - odd
                even = part(0)
                dbuf[1, f, version, c] = even + odd
                dbuf[2, f, version, c] = odd - even
                dbuf[3, f, version, c] = even - part(2)

    own_targets = (
        ((ROW0, None),),
        ((ROW1, None), (ROW1S, s1)),
        ((ROW2, None), (ROW2S, s2)),
        ((ROW3, None),),
    )

    def own(f, row):
        activate(f, xbuf.at[f, row], own_targets[row])

    def edge(f):
        activate(f, top.at[f], ((ABOVE, a0),))
        activate(f, bot.at[f], ((BELOW, live),))

    def add_weights(t, h):
        for c in range(chans // LANES):
            lanes = slice(c * LANES, (c + 1) * LANES)
            for r0 in range(0, chans, DEEP):
                at = slice(r0, r0 + DEEP)
                first, middle, final = [
                    wbuf[TAPS - 1 - t, h, k, at, lanes].astype(jnp.float32) for k in range(TAPS)
                ]
                both = first + final
                gbuf[0, t, h, c, at] = (both + middle).astype(jnp.bfloat16)
                gbuf[1, t, h, c, at] = (both - middle).astype(jnp.bfloat16)

    def across_lanes(ref):
        return jnp.concatenate([ref[c] for c in range(chans // LANES)], axis=1)

    def filters(p, t):
        if p in (0, 3):
            k = 0 if p == 0 else TAPS - 1
            return jnp.concatenate([wbuf[TAPS - 1 - t, h, k] for h in range(TAPS)], axis=0)
        return jnp.concatenate(
            [across_lanes(gbuf.at[p - 1, t, h]) for h in range(TAPS)], axis=0
        )

    written = set()

    def multiply(half, unit, p):
        sources, outputs, taps = UNITS[unit]
        left = jnp.concatenate(
            [
                jnp.concatenate(
                    [
                        across_lanes(dbuf.at[p, f, version])
                        for f in sources
                        for version in reads
                    ],
                    axis=1,
                )
                for reads in READS[half]
            ],
            axis=0,
        )
        right = jnp.concatenate(
            [
                jnp.concatenate([filters(p, t) for t in across], axis=1)
                if len(across) > 1 else filters(p, across[0])
                for across in taps
            ],
            axis=0,
        )
        product = jnp.dot(left, right, preferred_element_type=jnp.float32)
        for n, o in enumerate(outputs):
            part = product[:, n * chans : (n + 1) * chans]
            if (half, o, p) in written:
                ybuf[half, o, p] += part
            else:
                ybuf[half, o, p] = part
                written.add((half, o, p))

    oring = [0]

    def finish(half, f):
        for slot in range(2):
            row = ROW_OF[half][slot]
            b = oring[0] % RING
            oring[0] += 1
            at = slice(slot * half_w, (slot + 1) * half_w)
            for c in range(chans // LANES):
                lanes = slice(c * LANES, (c + 1) * LANES)
                y1, y2 = ybuf[half, f, 1, at, lanes], ybuf[half, f, 2, at, lanes]
                obuf[b, c, pl.ds(0, half_w, stride=2)] = (
                    ybuf[half, f, 0, at, lanes] + 0.5 * (y1 + y2)
                )
                obuf[b, c, pl.ds(1, half_w, stride=2)] = (
                    0.5 * (y1 - y2) - ybuf[half, f, 3, at, lanes]
                )
                total = obuf[b, c] + (
                    xbuf[f, row, :, lanes].astype(jnp.float32) + bias[:, lanes]
                )
                out_ref[f, row, :, lanes] = total.astype(jnp.bfloat16)

    rows = range(last + 1)

    def arrived(f):
        @pl.when(me > 0)
        def _():
            down(f).wait_recv()

        @pl.when(me < count - 1)
        def _():
            up(f).wait_recv()

    for f in range(2):
        x_copy(f).wait()
        for row in rows:
            own(f, row)
    x_copy(2).wait()
    w_copy(0).wait()
    w_copy(1).wait()
    multiply(0, C, 0)
    own(2, 0)
    own(2, 1)
    multiply(0, C, 3)
    own(2, 2)
    own(2, 3)
    multiply(0, B, 0)
    multiply(0, B, 3)
    for n in range(2, len(WPARTS)):
        w_copy(n).wait()
    multiply(0, A, 0)
    own(3, 0)
    own(3, 1)
    own(3, 2)
    own(3, 3)
    multiply(0, A, 3)
    for h in range(TAPS):
        add_weights(0, h)
    multiply(0, D, 0)
    add_weights(1, 0)
    multiply(0, D, 3)
    add_weights(1, 1)
    multiply(0, C, 1)
    add_weights(1, 2)
    multiply(0, C, 2)
    add_weights(2, 0)
    multiply(0, B, 1)
    add_weights(2, 1)
    multiply(0, B, 2)
    add_weights(2, 2)
    finish(0, 0)
    multiply(0, A, 1)
    multiply(0, A, 2)
    finish(0, 1)
    arrived(0)
    multiply(0, D, 1)
    edge(0)
    multiply(0, D, 2)
    for p in range(POINTS):
        multiply(1, C, p)
    edge(1)
    finish(0, 2)
    multiply(1, A, 0)
    finish(0, 3)
    multiply(1, A, 1)
    finish(1, 0)
    multiply(1, A, 2)
    multiply(1, A, 3)
    arrived(1)
    edge(2)
    multiply(1, B, 0)
    edge(3)
    multiply(1, B, 1)
    finish(1, 1)
    multiply(1, B, 2)
    multiply(1, B, 3)
    multiply(1, D, 0)
    finish(1, 2)
    multiply(1, D, 1)
    multiply(1, D, 2)
    multiply(1, D, 3)
    finish(1, 3)

    @pl.when(me < count - 1)
    def _():
        for n in range(frames // PAIR):
            down(n).wait_send()

    @pl.when(me > 0)
    def _():
        for n in range(frames // PAIR):
            up(n).wait_send()


def hand_on(frames, held, to_ref, sem):
    copies = [
        pltpu.make_async_copy(held.at[f], to_ref.at[f], sem.at[f])
        for f in range(frames)
    ]
    for copy in copies:
        copy.start()
    for copy in copies:
        copy.wait()


def per_device(latents, gamma, weight, bias, intersection, ramp):
    frames, rows, width, chans = latents.shape
    count = lax.axis_size("rows")
    hbm = pl.BlockSpec(memory_space=pltpu.HBM)
    vmem = pl.BlockSpec(memory_space=pltpu.VMEM)
    made = pl.pallas_call(
        functools.partial(kernel, frames, width, chans, count),
        out_shape=pltpu.VMEM(latents.shape, latents.dtype),
        in_specs=[hbm] * 6,
        out_specs=vmem,
        scratch_shapes=[
            pltpu.VMEM((frames, rows, width, chans), jnp.bfloat16),
            pltpu.VMEM((frames, width, chans), jnp.bfloat16),
            pltpu.VMEM((frames, width, chans), jnp.bfloat16),
            pltpu.VMEM((TAPS, TAPS, TAPS, chans, chans), jnp.bfloat16),
            pltpu.VMEM((2, TAPS, TAPS, chans // LANES, chans, LANES), jnp.bfloat16),
            pltpu.VMEM(
                (POINTS, frames, 8, chans // LANES, width // 2, LANES), jnp.bfloat16
            ),
            pltpu.VMEM((RING, chans // LANES, width + 2 * PAD, LANES), jnp.float32),
            pltpu.VMEM((2, frames, POINTS, width, chans), jnp.float32),
            pltpu.VMEM((RING, chans // LANES, width, LANES), jnp.float32),
            pltpu.VMEM(gamma.shape, jnp.float32),
            pltpu.VMEM(bias.shape, jnp.float32),
            pltpu.SMEM(intersection.shape, jnp.int32),
            pltpu.SMEM(ramp.shape, jnp.int32),
            pltpu.SemaphoreType.DMA((len(XPARTS),)),
            pltpu.SemaphoreType.DMA((len(WPARTS),)),
            pltpu.SemaphoreType.DMA((4,)),
            pltpu.SemaphoreType.DMA((2, frames // PAIR)),
            pltpu.SemaphoreType.DMA((2, frames // PAIR)),
        ],
        compiler_params=pltpu.CompilerParams(
            collective_id=0, has_side_effects=True, vmem_limit_bytes=56 * 1024 * 1024
        ),
    )(latents, weight, gamma, bias, intersection, ramp)
    return pl.pallas_call(
        functools.partial(hand_on, frames),
        out_shape=jax.ShapeDtypeStruct(latents.shape, latents.dtype),
        in_specs=[vmem],
        out_specs=hbm,
        scratch_shapes=[pltpu.SemaphoreType.DMA((frames,))],
        compiler_params=pltpu.CompilerParams(vmem_limit_bytes=16 * 1024 * 1024),
    )(made)


def solution(mesh):
    in_specs = (P("clips", "rows", None, None), P(), P(), P(), P("clips"), P("clips"))
    out_specs = P("clips", "rows", None, None)
    return jax.shard_map(
        per_device, mesh=mesh, in_specs=in_specs, out_specs=out_specs, check_vma=False
    )
```

```python
import functools

import jax
import jax.numpy as jnp
from jax import lax
from jax.experimental import pallas as pl
from jax.experimental.pallas import tpu as pltpu
from jax.sharding import PartitionSpec as P

TAPS = 3
POINTS = 4
MESH = pl.DeviceIdType.MESH
PAD = 8
LANES = 128
RING = 8

ABOVE, ROW0, ROW1, ROW1S, ROW2, ROW2S, ROW3, BELOW = range(8)
ROW_OF = ((1, 2), (0, 3))
READS = (
    ((ROW0, ROW1, ROW2S), (ROW1, ROW2, ROW3)),
    ((ABOVE, ROW0, ROW1S), (ROW2, ROW3, BELOW)),
)
UNITS = (
    ((1, 0), (1, 2), ((0, 1), (1, 2))),
    ((2,), (2, 3), ((0, 1),)),
    ((0,), (0,), ((0,),)),
    ((1, 3), (3,), ((2,), (0,))),
)
A, B, C, D = range(4)
STEP = 32
DEEP = 64
XPARTS = (pl.ds(0, 1), pl.ds(1, 1), pl.ds(2, 2))
WPARTS = (
    (pl.ds(1, 2), 0), (pl.ds(1, 2), 2), (pl.ds(0, 1), 0), (pl.ds(0, 1), 2),
    (pl.ds(0, TAPS), 1),
)
PAIR = 2


def kernel(
    frames, width, chans, count,
    x_ref, w_ref, gamma_hbm, bias_hbm, inter_hbm, ramp_hbm,
    out_ref,
    xbuf, top, bot, wbuf, gbuf, dbuf, act, ybuf, obuf, gamma_ref, bias_ref, inter_ref, ramp_ref,
    xsem, wsem, ssem, send_sem, recv_sem,
):
    me = lax.axis_index("rows")
    last = xbuf.shape[1] - 1
    half_w = width // 2

    def x_copy(n):
        at = XPARTS[n]
        return pltpu.make_async_copy(x_ref.at[at], xbuf.at[at], xsem.at[n])

    def w_copy(n):
        t, k = WPARTS[n]
        return pltpu.make_async_copy(w_ref.at[t, :, k], wbuf.at[t, :, k], wsem.at[n])

    def down(n):
        at = pl.ds(n * PAIR, PAIR)
        return pltpu.make_async_remote_copy(
            src_ref=x_ref.at[at, last], dst_ref=top.at[at],
            send_sem=send_sem.at[0, n], recv_sem=recv_sem.at[0, n],
            device_id={"rows": me + 1}, device_id_type=MESH,
        )

    def up(n):
        at = pl.ds(n * PAIR, PAIR)
        return pltpu.make_async_remote_copy(
            src_ref=x_ref.at[at, 0], dst_ref=bot.at[at],
            send_sem=send_sem.at[1, n], recv_sem=recv_sem.at[1, n],
            device_id={"rows": me - 1}, device_id_type=MESH,
        )

    small = (
        pltpu.make_async_copy(inter_hbm, inter_ref, ssem.at[0]),
        pltpu.make_async_copy(ramp_hbm, ramp_ref, ssem.at[1]),
        pltpu.make_async_copy(gamma_hbm, gamma_ref, ssem.at[2]),
        pltpu.make_async_copy(bias_hbm, bias_ref, ssem.at[3]),
    )
    barrier = pltpu.get_barrier_semaphore()

    @pl.when(me > 0)
    def _():
        pl.semaphore_signal(
            barrier, inc=1, device_id={"rows": me - 1}, device_id_type=MESH
        )

    @pl.when(me < count - 1)
    def _():
        pl.semaphore_signal(
            barrier, inc=1, device_id={"rows": me + 1}, device_id_type=MESH
        )

    for copy in small:
        copy.start()
    for n in range(len(XPARTS)):
        x_copy(n).start()
    for n in range(len(WPARTS)):
        w_copy(n).start()

    @pl.when(me == 0)
    def _():
        top[...] = jnp.zeros(top.shape, top.dtype)

    @pl.when(me == count - 1)
    def _():
        bot[...] = jnp.zeros(bot.shape, bot.dtype)

    for b in range(RING):
        for c in range(chans // LANES):
            act[b, c, 0:PAD] = jnp.zeros((PAD, LANES), jnp.float32)
            act[b, c, PAD + width : PAD + width + PAD] = jnp.zeros(
                (PAD, LANES), jnp.float32
            )

    peers = jnp.where(me > 0, 1, 0) + jnp.where(me < count - 1, 1, 0)
    pl.semaphore_wait(barrier, peers)

    for n in range(frames // PAIR):

        @pl.when(me < count - 1)
        def _():
            down(n).start()

        @pl.when(me > 0)
        def _():
            up(n).start()

    for copy in small:
        copy.wait()

    before = jnp.maximum(me - 1, 0)
    prev_ov = jnp.where(me > 0, inter_ref[before], 0)
    own_ov = jnp.where(me == count - 1, 0, inter_ref[me])
    ovv = jnp.full((1, chans), prev_ov, jnp.int32)
    ownv = jnp.full((1, chans), own_ov, jnp.int32)
    rampv = jnp.full((1, chans), ramp_ref[before], jnp.int32).astype(jnp.float32)
    a0 = jnp.where(ovv > 0, jnp.maximum(rampv, 0.0) / (rampv + 1.0), 0.0)
    a1 = jnp.where(ovv > 1, jnp.maximum(rampv - 1.0, 0.0) / (rampv + 1.0), 0.0)
    s1 = jnp.where(ovv > 1, 1.0, 1.0 - a0)
    s2 = 1.0 - a1
    live = jnp.where(ownv > 0, 1.0, 0.0)
    half_gamma = 0.5 * gamma_ref[...].reshape(1, chans)
    bias = bias_ref[...].reshape(1, chans)
    ring = [0]

    def activate(f, source, targets):
        b = ring[0] % RING
        ring[0] += 1
        for w0 in range(0, width, STEP):
            values = source[w0 : w0 + STEP].astype(jnp.float32)
            square = jnp.mean(values * values, axis=-1, keepdims=True)
            half = values * lax.rsqrt(square + 1e-06) * half_gamma
            value = half + half * jnp.tanh(half)
            for c in range(chans // LANES):
                lanes = slice(c * LANES, (c + 1) * LANES)
                act[b, c, PAD + w0 : PAD + w0 + STEP] = value[:, lanes]
        for c in range(chans // LANES):
            lanes = slice(c * LANES, (c + 1) * LANES)
            for version, scale in targets:

                def part(at):
                    one = act[b, c, pl.ds(PAD + at, half_w, stride=2)]
                    if scale is not None:
                        one = one * scale[:, lanes]
                    return one.astype(jnp.bfloat16)

                odd = part(1)
                dbuf[0, f, version, c] = part(-1) - odd
                even = part(0)
                dbuf[1, f, version, c] = even + odd
                dbuf[2, f, version, c] = odd - even
                dbuf[3, f, version, c] = even - part(2)

    own_targets = (
        ((ROW0, None),),
        ((ROW1, None), (ROW1S, s1)),
        ((ROW2, None), (ROW2S, s2)),
        ((ROW3, None),),
    )

    def own(f, row):
        activate(f, xbuf.at[f, row], own_targets[row])

    def edge(f):
        activate(f, top.at[f], ((ABOVE, a0),))
        activate(f, bot.at[f], ((BELOW, live),))

    def add_weights(t, h):
        for c in range(chans // LANES):
            lanes = slice(c * LANES, (c + 1) * LANES)
            for r0 in range(0, chans, DEEP):
                at = slice(r0, r0 + DEEP)
                first, middle, final = [
                    wbuf[TAPS - 1 - t, h, k, at, lanes].astype(jnp.float32) for k in range(TAPS)
                ]
                both = first + final
                gbuf[0, t, h, c, at] = (both + middle).astype(jnp.bfloat16)
                gbuf[1, t, h, c, at] = (both - middle).astype(jnp.bfloat16)

    def across_lanes(ref):
        return jnp.concatenate([ref[c] for c in range(chans // LANES)], axis=1)

    def filters(p, t):
        if p in (0, 3):
            k = 0 if p == 0 else TAPS - 1
            return jnp.concatenate([wbuf[TAPS - 1 - t, h, k] for h in range(TAPS)], axis=0)
        return jnp.concatenate(
            [across_lanes(gbuf.at[p - 1, t, h]) for h in range(TAPS)], axis=0
        )

    written = set()

    def multiply(half, unit, p):
        sources, outputs, taps = UNITS[unit]
        left = jnp.concatenate(
            [
                jnp.concatenate(
                    [
                        across_lanes(dbuf.at[p, f, version])
                        for f in sources
                        for version in reads
                    ],
                    axis=1,
                )
                for reads in READS[half]
            ],
            axis=0,
        )
        right = jnp.concatenate(
            [
                jnp.concatenate([filters(p, t) for t in across], axis=1)
                if len(across) > 1 else filters(p, across[0])
                for across in taps
            ],
            axis=0,
        )
        product = jnp.dot(left, right, preferred_element_type=jnp.float32)
        for n, o in enumerate(outputs):
            part = product[:, n * chans : (n + 1) * chans]
            if (half, o, p) in written:
                ybuf[half, o, p] += part
            else:
                ybuf[half, o, p] = part
                written.add((half, o, p))

    oring = [0]

    def finish(half, f):
        for slot in range(2):
            row = ROW_OF[half][slot]
            b = oring[0] % RING
            oring[0] += 1
            at = slice(slot * half_w, (slot + 1) * half_w)
            for c in range(chans // LANES):
                lanes = slice(c * LANES, (c + 1) * LANES)
                y1, y2 = ybuf[half, f, 1, at, lanes], ybuf[half, f, 2, at, lanes]
                obuf[b, c, pl.ds(0, half_w, stride=2)] = (
                    ybuf[half, f, 0, at, lanes] + 0.5 * (y1 + y2)
                )
                obuf[b, c, pl.ds(1, half_w, stride=2)] = (
                    0.5 * (y1 - y2) - ybuf[half, f, 3, at, lanes]
                )
                total = obuf[b, c] + (
                    xbuf[f, row, :, lanes].astype(jnp.float32) + bias[:, lanes]
                )
                out_ref[f, row, :, lanes] = total.astype(jnp.bfloat16)

    rows = range(last + 1)

    def arrived(f):
        @pl.when(me > 0)
        def _():
            down(f).wait_recv()

        @pl.when(me < count - 1)
        def _():
            up(f).wait_recv()

    for f in range(2):
        x_copy(f).wait()
        for row in rows:
            own(f, row)
    x_copy(2).wait()
    own(2, 0)
    own(2, 1)
    w_copy(0).wait()
    w_copy(1).wait()
    multiply(0, C, 0)
    own(2, 2)
    own(2, 3)
    multiply(0, C, 3)
    own(3, 0)
    multiply(0, B, 0)
    own(3, 1)
    multiply(0, B, 3)
    for n in range(2, len(WPARTS)):
        w_copy(n).wait()
    multiply(0, A, 0)
    own(3, 2)
    own(3, 3)
    multiply(0, A, 3)
    for h in range(TAPS):
        add_weights(0, h)
    multiply(0, D, 0)
    add_weights(1, 0)
    multiply(0, D, 3)
    add_weights(1, 1)
    multiply(0, C, 1)
    add_weights(1, 2)
    multiply(0, C, 2)
    add_weights(2, 0)
    multiply(0, B, 1)
    add_weights(2, 1)
    multiply(0, B, 2)
    add_weights(2, 2)
    finish(0, 0)
    multiply(0, A, 1)
    multiply(0, A, 2)
    finish(0, 1)
    arrived(0)
    multiply(0, D, 1)
    edge(0)
    multiply(0, D, 2)
    for p in range(POINTS):
        multiply(1, C, p)
    edge(1)
    finish(0, 2)
    multiply(1, A, 0)
    finish(0, 3)
    multiply(1, A, 1)
    finish(1, 0)
    multiply(1, A, 2)
    multiply(1, A, 3)
    arrived(1)
    edge(2)
    multiply(1, B, 0)
    edge(3)
    multiply(1, B, 1)
    finish(1, 1)
    multiply(1, B, 2)
    multiply(1, B, 3)
    multiply(1, D, 0)
    finish(1, 2)
    multiply(1, D, 1)
    multiply(1, D, 2)
    multiply(1, D, 3)
    finish(1, 3)

    @pl.when(me < count - 1)
    def _():
        for n in range(frames // PAIR):
            down(n).wait_send()

    @pl.when(me > 0)
    def _():
        for n in range(frames // PAIR):
            up(n).wait_send()


def hand_on(frames, held, to_ref, sem):
    copies = [
        pltpu.make_async_copy(held.at[f], to_ref.at[f], sem.at[f])
        for f in range(frames)
    ]
    for copy in copies:
        copy.start()
    for copy in copies:
        copy.wait()


def per_device(latents, gamma, weight, bias, intersection, ramp):
    frames, rows, width, chans = latents.shape
    count = lax.axis_size("rows")
    hbm = pl.BlockSpec(memory_space=pltpu.HBM)
    vmem = pl.BlockSpec(memory_space=pltpu.VMEM)
    made = pl.pallas_call(
        functools.partial(kernel, frames, width, chans, count),
        out_shape=pltpu.VMEM(latents.shape, latents.dtype),
        in_specs=[hbm] * 6,
        out_specs=vmem,
        scratch_shapes=[
            pltpu.VMEM((frames, rows, width, chans), jnp.bfloat16),
            pltpu.VMEM((frames, width, chans), jnp.bfloat16),
            pltpu.VMEM((frames, width, chans), jnp.bfloat16),
            pltpu.VMEM((TAPS, TAPS, TAPS, chans, chans), jnp.bfloat16),
            pltpu.VMEM((2, TAPS, TAPS, chans // LANES, chans, LANES), jnp.bfloat16),
            pltpu.VMEM(
                (POINTS, frames, 8, chans // LANES, width // 2, LANES), jnp.bfloat16
            ),
            pltpu.VMEM((RING, chans // LANES, width + 2 * PAD, LANES), jnp.float32),
            pltpu.VMEM((2, frames, POINTS, width, chans), jnp.float32),
            pltpu.VMEM((RING, chans // LANES, width, LANES), jnp.float32),
            pltpu.VMEM(gamma.shape, jnp.float32),
            pltpu.VMEM(bias.shape, jnp.float32),
            pltpu.SMEM(intersection.shape, jnp.int32),
            pltpu.SMEM(ramp.shape, jnp.int32),
            pltpu.SemaphoreType.DMA((len(XPARTS),)),
            pltpu.SemaphoreType.DMA((len(WPARTS),)),
            pltpu.SemaphoreType.DMA((4,)),
            pltpu.SemaphoreType.DMA((2, frames // PAIR)),
            pltpu.SemaphoreType.DMA((2, frames // PAIR)),
        ],
        compiler_params=pltpu.CompilerParams(
            collective_id=0, has_side_effects=True, vmem_limit_bytes=56 * 1024 * 1024
        ),
    )(latents, weight, gamma, bias, intersection, ramp)
    return pl.pallas_call(
        functools.partial(hand_on, frames),
        out_shape=jax.ShapeDtypeStruct(latents.shape, latents.dtype),
        in_specs=[vmem],
        out_specs=hbm,
        scratch_shapes=[pltpu.SemaphoreType.DMA((frames,))],
        compiler_params=pltpu.CompilerParams(vmem_limit_bytes=16 * 1024 * 1024),
    )(made)


def solution(mesh):
    in_specs = (P("clips", "rows", None, None), P(), P(), P(), P("clips"), P("clips"))
    out_specs = P("clips", "rows", None, None)
    return jax.shard_map(
        per_device, mesh=mesh, in_specs=in_specs, out_specs=out_specs, check_vma=False
    )
```
